32 devices in a mesh: grp: 4 (over y, x), dev: 8 (over z, core).
Axes of the slice: x: 2, y: 2, z: 4, core: 2. Of those that a mesh axis runs over, the one named last changes fastest.
Arguments:
- ref_volume: bfloat16 [256, 128, 1024], P('dev', None, 'grp'), may hold values from -6 to 6
- def_volume: bfloat16 [256, 128, 1024], P('dev', None, 'grp'), may hold values from -6 to 6
- shifts: int32 [4, 8], P('grp', 'dev'), may hold values from -8 to 8, as said below
- init_disp: float32 [3, 17, 9, 65], replicated, may hold values from -3 to 3
- precond: float32 [3, 17, 9, 65], replicated, may hold values from 0.001 to 0.01
Outputs:
- displacement: float32 [3, 17, 9, 65], replicated
- residual: float32 [256, 128, 1024], P('dev', None, 'grp')
- misfit: float32 [], replicated
The draws below stay inside these ranges and needn't reach their ends.
Inputs may be any that keep to these rules, and one draw needn't show every extreme that they name: `shifts`: every entry lies within 8 in magnitude; both 8 and -8 occur in every draw.
All inputs are finite; a program needn't handle non-finite values.
Results may differ from the reference program's by a relative error of at most 0.0003.
Values may be sent and summed in bfloat16 or wider, within the bound.
A program may use at most 128 MiB of HBM per device.

```python
import math
import jax
import jax.numpy as jnp
from jax import lax

E = 16
SMAX = 8
ITERS = 2
BX = 32
YW = 128
BZ = 256
GROUPS = 4
BRICKS = 8
NX = 256
NZ = 1024
NODES_X = 17
NODES_Y = 9
NODES_Z = 65
NODES_BX = 3
NODES_BZ = 17


def draw_shifts(key, part):
    base = jax.random.randint(jax.random.fold_in(key, 11), (GROUPS * BRICKS,), -SMAX, SMAX + 1)
    order = jax.random.permutation(jax.random.fold_in(key, 12), GROUPS * BRICKS)
    base = base.at[order[0]].set(SMAX)
    base = base.at[order[1]].set(-SMAX)
    return base.reshape(GROUPS, BRICKS).astype(jnp.int32)


def rising_scale(key):
    along_x = (jnp.arange(NX, dtype=jnp.float32) + 0.5) / NX
    along_z = (jnp.arange(NZ, dtype=jnp.float32) + 0.5) / NZ
    extra_x = jnp.zeros((), jnp.float32)
    extra_z = jnp.zeros((), jnp.float32)
    grow_x = jnp.exp((1.0986123 + extra_x) * along_x)
    grow_z = jnp.exp((1.0986123 + extra_z) * along_z)
    return grow_x[:, None, None] * grow_z[None, None, :]


def textured(key, salt):
    shape = (NX, YW, NZ)
    cells = (NX // 8, YW // 8, NZ // 8)
    base = jax.random.truncated_normal(jax.random.fold_in(key, salt + 3), -3.5, 3.5, shape, jnp.float32)
    level = jax.random.uniform(jax.random.fold_in(key, salt + 4), cells, jnp.float32, -0.4, 0.4)
    start = 0.45
    mixed = (base + jnp.roll(base, (1, 1), axis=(0, 1))) * 0.70710678
    amplitude = jnp.exp(level)
    amplitude = jnp.repeat(jnp.repeat(jnp.repeat(amplitude, 8, axis=0), 8, axis=1), 8, axis=2)
    scale = start * rising_scale(key)
    return jnp.clip(mixed * amplitude * scale, -6.0, 6.0).astype(jnp.bfloat16)


def draw_def_volume(key, part):
    return textured(key, 20)


def draw_ref_volume(key, part):
    return textured(key, 40)


def draw_init_disp(key, part):
    shape = (NODES_X, NODES_Y, NODES_Z)
    common = 0.4 * jax.random.normal(jax.random.fold_in(key, 35), shape, jnp.float32)
    noise_x = 0.3 * jax.random.normal(jax.random.fold_in(key, 36), shape, jnp.float32)
    noise_y = 0.3 * jax.random.normal(jax.random.fold_in(key, 37), shape, jnp.float32)
    along_z = 0.5 * jax.random.normal(jax.random.fold_in(key, 38), shape, jnp.float32)
    stacked = jnp.stack([common + noise_x, noise_y - common, along_z])
    return jnp.clip(stacked, -3.0, 3.0).astype(jnp.float32)


def setup_inputs(seed: int = 0) -> dict:
    arg_keys = jax.random.split(jax.random.key(seed), 6)
    ref_volume = draw_ref_volume(jax.random.fold_in(arg_keys[5], 71), 0)
    def_volume = draw_def_volume(jax.random.fold_in(arg_keys[5], 71), 0)
    shifts = draw_shifts(jax.random.fold_in(arg_keys[5], 71), 0)
    init_disp = draw_init_disp(jax.random.fold_in(arg_keys[5], 71), 0)
    precond = jnp.clip(jnp.exp(jax.random.uniform(arg_keys[4], (3, NODES_X, NODES_Y, NODES_Z), jnp.float32, math.log(0.001), math.log(0.01))), 0.001, 0.01)
    return {"ref_volume": ref_volume, "def_volume": def_volume, "shifts": shifts, "init_disp": init_disp, "precond": precond}


epsilon = 1e-06

def hat_matrix(voxels, nodes):
    positions = jnp.arange(voxels, dtype=jnp.int32)
    element = positions // E
    fraction = (positions - element * E).astype(jnp.float32) / E
    columns = jnp.arange(nodes, dtype=jnp.int32)
    left_part = (columns[None, :] == element[:, None]).astype(jnp.float32) * (1.0 - fraction)[:, None]
    right_part = (columns[None, :] == element[:, None] + 1).astype(jnp.float32) * fraction[:, None]
    return left_part + right_part

def smooth(values, direction):
    extent = values.shape[direction]
    lower = lax.slice_in_dim(values, 0, extent - 2, axis=direction)
    middle = lax.slice_in_dim(values, 1, extent - 1, axis=direction)
    upper = lax.slice_in_dim(values, 2, extent, axis=direction)
    return (lower + 4.0 * middle + upper) / 6.0

def differ(values, direction):
    extent = values.shape[direction]
    lower = lax.slice_in_dim(values, 0, extent - 2, axis=direction)
    upper = lax.slice_in_dim(values, 2, extent, axis=direction)
    return 0.5 * (upper - lower)

def gradients(window):
    smooth_z = smooth(window, 2)
    slope_x = differ(smooth(smooth_z, 1), 0)
    slope_y = smooth(differ(smooth_z, 1), 0)
    slope_z = smooth(smooth(differ(window, 2), 1), 0)
    return jnp.stack([slope_x, slope_y, slope_z])

def interpolate(local_nodes, hat_x, hat_y, hat_z):
    highest = lax.Precision.HIGHEST
    partial_z = jnp.einsum('cijk,zk->cijz', local_nodes, hat_z, precision=highest)
    partial_y = jnp.einsum('cijz,yj->ciyz', partial_z, hat_y, precision=highest)
    return jnp.einsum('ciyz,xi->cxyz', partial_y, hat_x, precision=highest)

def restrict(terms, hat_x, hat_y, hat_z):
    highest = lax.Precision.HIGHEST
    partial_x = jnp.einsum('cxyz,xi->ciyz', terms, hat_x, precision=highest)
    partial_y = jnp.einsum('ciyz,yj->cijz', partial_x, hat_y, precision=highest)
    return jnp.einsum('cijz,zk->cijk', partial_y, hat_z, precision=highest)

def reference(ref_volume, def_volume, shifts, init_disp, precond):
    margin = SMAX + 1
    padded = jnp.pad(def_volume, ((margin, margin), (1, 1), (1, 1)))
    voxel_count = float(NX * YW * NZ)
    target_all = ref_volume.astype(jnp.float32)
    mean_ref = jnp.sum(target_all) / voxel_count
    var_ref = jnp.sum(target_all * target_all) / voxel_count - mean_ref * mean_ref
    hat_x = hat_matrix(BX, NODES_BX)
    hat_y = hat_matrix(YW, NODES_Y)
    hat_z = hat_matrix(BZ, NODES_BZ)
    brick_ids = jnp.arange(GROUPS * BRICKS, dtype=jnp.int32)
    zero_index = jnp.zeros((), jnp.int32)

    def corner_of(brick):
        group_index = (brick // BRICKS).astype(jnp.int32)
        brick_index = (brick % BRICKS).astype(jnp.int32)
        return (group_index, brick_index)

    def state(motion, brick):
        group_index, brick_index = corner_of(brick)
        offset = shifts[group_index, brick_index].astype(jnp.int32)
        start_x = (brick_index * BX + offset + margin - 1).astype(jnp.int32)
        start_z = (group_index * BZ).astype(jnp.int32)
        window = lax.dynamic_slice(padded, (start_x, zero_index, start_z), (BX + 2, YW + 2, BZ + 2)).astype(jnp.float32)
        slopes = gradients(window)
        sample = window[1:-1, 1:-1, 1:-1]
        node_x = (brick_index * (BX // E)).astype(jnp.int32)
        node_z = (group_index * (BZ // E)).astype(jnp.int32)
        local_nodes = lax.dynamic_slice(motion, (zero_index, node_x, zero_index, node_z), (3, NODES_BX, NODES_Y, NODES_BZ))
        shift_field = interpolate(local_nodes, hat_x, hat_y, hat_z)
        warped = sample + lax.optimization_barrier(jnp.sum(shift_field * slopes, axis=0))
        target = lax.dynamic_slice(ref_volume, ((brick_index * BX).astype(jnp.int32), zero_index, start_z), (BX, YW, BZ)).astype(jnp.float32)
        return (warped, slopes, target)
    motion = init_disp
    residuals = None
    squares = None
    for iteration in range(ITERS):

        def moments(brick):
            warped, slopes, target = state(motion, brick)
            return jnp.stack([jnp.sum(warped), jnp.sum(warped * warped)])
        totals = lax.optimization_barrier(jnp.sum(lax.map(moments, brick_ids), axis=0))
        mean_img = totals[0] / voxel_count
        var_img = totals[1] / voxel_count - mean_img * mean_img
        ratio = jnp.sqrt((var_ref + epsilon) / (var_img + epsilon))

        def forces_of(brick):
            warped, slopes, target = state(motion, brick)
            residual_brick = target - mean_ref - ratio * (warped - mean_img)
            slab = restrict(slopes * residual_brick[None], hat_x, hat_y, hat_z)
            return (slab, residual_brick, jnp.sum(residual_brick * residual_brick))
        slabs, residuals, squares = lax.map(forces_of, brick_ids)

        def add_slab(brick, total):
            group_index, brick_index = corner_of(brick)
            corner = (zero_index, (brick_index * (BX // E)).astype(jnp.int32), zero_index, (group_index * (BZ // E)).astype(jnp.int32))
            current = lax.dynamic_slice(total, corner, (3, NODES_BX, NODES_Y, NODES_BZ))
            return lax.dynamic_update_slice(total, current + slabs[brick], corner)
        forces = lax.fori_loop(jnp.int32(0), jnp.int32(GROUPS * BRICKS), add_slab, jnp.zeros((3, NODES_X, NODES_Y, NODES_Z), jnp.float32))
        motion = motion + precond * forces
    residual_field = residuals.reshape(GROUPS, BRICKS, BX, YW, BZ).transpose(1, 2, 3, 0, 4).reshape(NX, YW, NZ)
    misfit = jnp.sqrt(jnp.sum(squares) / voxel_count)
    return (motion, residual_field, misfit)
```

```python
import functools

import jax
import jax.numpy as jnp
from jax import lax
from jax.experimental import pallas as pl
from jax.experimental.pallas import tpu as pltpu
from jax.sharding import PartitionSpec as P

E = 16
SMAX = 8
MARGIN = SMAX + 1
EPS = 1e-06
F32 = jnp.float32
BF16 = jnp.bfloat16
HIGHEST = lax.Precision.HIGHEST
MESH = pl.DeviceIdType.MESH


def iota(shape, dim):
    return lax.broadcasted_iota(jnp.int32, shape, dim)


def dot(a, b):
    return jnp.dot(a, b, preferred_element_type=F32)


def split_dot_left(a, b):
    high = a.astype(BF16)
    low = (a - high.astype(F32)).astype(BF16)
    return dot(high, b) + dot(low, b)


def split_dot_right(a, b):
    high = b.astype(BF16)
    low = (b - high.astype(F32)).astype(BF16)
    return dot(a, high) + dot(a, low)


def hat(distance):
    return jnp.maximum(1.0 - jnp.abs(distance).astype(F32) / E, 0.0)


def kernel(
    grps, devs, ref_hbm, def_hbm, faces, shifts, init, precond,
    disp, res_hbm, misfit,
    ref_v, wide, face_b, face_f, turned, target, pa, pb, pc, image, field, fine, nodes, bands, offs,
    slab, packs, stats, nbuf, gbuf, dbuf,
    sem_loc, sem_hs, sem_hr, sem_fs, sem_fr, sem_ss, sem_sr, sem_ns, sem_nr, sem_gs, sem_gr, sem_ds, sem_dr, sem_out,
):
    width, rows, depth = ref_v.shape
    nodes_y, nodes_z = init.shape[2:]
    total = grps * devs
    count = float(total * width * rows * depth)
    gi, di = lax.axis_index("grp"), lax.axis_index("dev")
    me = gi * devs + di

    def place(peer):
        return (peer // devs, lax.rem(peer, devs))

    def exists(dg, dd):
        g, d = gi + dg, di + dd
        return (g >= 0) & (g < grps) & (d >= 0) & (d < devs)

    def remote(src, dst, ss, rs, g, d):
        return pltpu.make_async_remote_copy(
            src_ref=src, dst_ref=dst, send_sem=ss, recv_sem=rs, device_id=(g, d), device_id_type=MESH
        )

    load_def = pltpu.make_async_copy(def_hbm, wide.at[pl.ds(MARGIN, width)], sem_loc.at[0])
    load_ref = pltpu.make_async_copy(ref_hbm, ref_v, sem_loc.at[1])
    load_def.start()
    load_ref.start()

    barrier = pltpu.get_barrier_semaphore()

    def greet(k, carry):
        pl.semaphore_signal(barrier, inc=1, device_id=place(lax.rem(me + k, total)), device_id_type=MESH)
        return carry

    lax.fori_loop(1, total, greet, 0)
    pl.semaphore_wait(barrier, total - 1)

    to_right = remote(
        def_hbm.at[pl.ds(width - MARGIN, MARGIN)], wide.at[pl.ds(0, MARGIN)],
        sem_hs.at[0], sem_hr.at[0], gi, di + 1,
    )
    to_left = remote(
        def_hbm.at[pl.ds(0, MARGIN)], wide.at[pl.ds(MARGIN + width, MARGIN)],
        sem_hs.at[1], sem_hr.at[1], gi, di - 1,
    )
    has_left, has_right = di > 0, di < devs - 1

    @pl.when(has_right)
    def _():
        to_right.start()

    @pl.when(has_left)
    def _():
        to_left.start()

    face_moves = []
    for dg in (1, -1):
        for dd in (-1, 0, 1):
            side = 0 if dg == 1 else 1
            slot = 1 - dd
            copy = remote(
                faces.at[1 - side], face_b.at[side, slot],
                sem_fs.at[side, slot], sem_fr.at[side, slot], gi + dg, di + dd,
            )
            face_moves.append((dg, dd, copy))

            @pl.when(exists(dg, dd))
            def _(copy=copy):
                copy.start()

            @pl.when(jnp.logical_not(exists(-dg, -dd)))
            def _(side=side, slot=slot):
                face_b[side, slot] = jnp.zeros((width, rows), BF16)

    @pl.when(jnp.logical_not(has_left))
    def _():
        wide[pl.ds(0, MARGIN)] = jnp.zeros((MARGIN, rows, depth), BF16)

    @pl.when(jnp.logical_not(has_right))
    def _():
        wide[pl.ds(MARGIN + width, MARGIN)] = jnp.zeros((MARGIN, rows, depth), BF16)

    k, j = iota((depth, 2 * depth), 0), iota((depth, 2 * depth), 1)
    is_d = j >= depth
    gap = k - jnp.where(is_d, j - depth, j)
    smooth_w = jnp.where(gap == 0, 4.0, jnp.where(jnp.abs(gap) == 1, 1.0, 0.0))
    differ_w = jnp.where(jnp.abs(gap) == 1, gap, 0).astype(F32)
    bands[...] = jnp.where(is_d, differ_w, smooth_w).astype(BF16)
    k, j = iota((128, 2 * depth), 0), iota((128, 2 * depth), 1)
    low = (j == 0) | (j == depth)
    high = (j == depth - 1) | (j == 2 * depth - 1)
    offs[...] = jnp.where(low, k, jnp.where(high, k - 64, -1))

    nodes[...] = jnp.zeros_like(nodes)
    z_of = iota((128, depth), 1) + gi * depth
    hat_up = hat(z_of - E * iota((128, depth), 0))
    hat_y = hat(iota((rows, 16), 0) - E * iota((rows, 16), 1))

    def expand():
        along_z = jnp.dot(nodes[...], hat_up, preferred_element_type=F32, precision=HIGHEST) * (1.0 / 72.0)
        for m in range(9):
            fine[m] = jnp.dot(
                hat_y, along_z[16 * m : 16 * m + 16], preferred_element_type=F32, precision=HIGHEST
            )

    for c in range(3):
        for n in range(3):
            m = 3 * c + n
            nodes[16 * m : 16 * m + nodes_y, 0:nodes_z] = init[c, 2 * di + n]
    expand()

    load_ref.wait()

    def convert(x, carry):
        s0, s1 = carry
        t = ref_v[x].astype(F32)
        target[x] = t
        t = t.reshape(rows // 8, 8, depth)
        return s0 + jnp.sum(t, axis=0), s1 + jnp.sum(t * t, axis=0)

    zero = jnp.zeros((8, depth), F32)
    sum_t, sum_tt = lax.fori_loop(0, width, convert, (zero, zero))

    load_def.wait()

    @pl.when(has_right)
    def _():
        to_right.wait_send()
        to_left.wait_recv()

    @pl.when(has_left)
    def _():
        to_left.wait_send()
        to_right.wait_recv()

    for dg, dd, copy in face_moves:

        @pl.when(exists(dg, dd))
        def _(copy=copy):
            copy.wait_send()

        @pl.when(exists(-dg, -dd))
        def _(copy=copy):
            copy.wait_recv()

    shift = shifts[0, 0]
    for side in range(2):
        for slot in range(3):
            face_f[side, pl.ds(slot * width, width)] = face_b[side, slot].astype(F32)
    low_rows = face_f[0, pl.ds(width - 1 + shift, 40)]
    high_rows = face_f[1, pl.ds(width - 1 + shift, 40)]
    gap_rows = jnp.zeros((24, rows), F32)
    stacked = jnp.concatenate([low_rows, gap_rows, high_rows, gap_rows], axis=0)
    turned[...] = jnp.transpose(stacked).astype(BF16)

    row = iota((rows, depth), 0)
    column = iota((128, 2 * depth), 1)
    sign = jnp.where(column == depth, -1.0, 1.0)

    def gradient(x, carry):
        plane = wide[x + shift + SMAX]
        pick = jnp.where(offs[...] == x, sign, 0.0).astype(BF16)
        both = dot(plane, bands[...]) + dot(turned[...], pick)
        sz, dz = both[:, :depth], both[:, depth:]
        s_prev = jnp.where(row == 0, 0.0, pltpu.roll(sz, 1, 0))
        s_next = jnp.where(row == rows - 1, 0.0, pltpu.roll(sz, rows - 1, 0))
        d_prev = jnp.where(row == 0, 0.0, pltpu.roll(dz, 1, 0))
        d_next = jnp.where(row == rows - 1, 0.0, pltpu.roll(dz, rows - 1, 0))
        pa[x] = s_prev + s_next + 4.0 * sz
        pb[x] = s_next - s_prev
        pc[x] = d_prev + d_next + 4.0 * dz
        image[x] = plane.astype(F32)
        return carry

    lax.fori_loop(0, width + 2, gradient, 0)

    tile = (8, 128)
    lanes = depth // 128
    chunks = (rows // 8) * lanes

    def chunk_at(q):
        return pl.ds(pl.multiple_of((q // lanes) * 8, 8), 8), pl.ds(pl.multiple_of(lax.rem(q, lanes) * 128, 128), 128)

    def finish(e, base, sums, ry, rz):
        for m, (s0, s1) in enumerate(sums):
            s1 = s1 * (1.0 / E)
            f = base + m
            if e == 1:
                field[3 * f + 2, ry, rz] = s1
                field[3 * f + 1, ry, rz] = s0 - s1
            else:
                field[3 * f + 1, ry, rz] += s1
                field[3 * f, ry, rz] = s0 - s1

    zt = jnp.zeros(tile, F32)

    def pass_one(e):
        def body(q, carry):
            sw, sww = carry
            ry, rz = chunk_at(q)
            here = [fine[3 * c + e + 1, ry, rz] for c in range(3)]
            step = [(here[c] - fine[3 * c + e, ry, rz]) * (1.0 / E) for c in range(3)]
            sums = [(zt, zt)] * 9
            top = E * e + E + 1
            a1, a2 = pa[top - 1, ry, rz], pa[top, ry, rz]
            b1, b2 = pb[top - 1, ry, rz], pb[top, ry, rz]
            c1, c2 = pc[top - 1, ry, rz], pc[top, ry, rz]
            for i in range(E - 1, -1, -1):
                x = E * e + i
                a0, b0, c0 = pa[x, ry, rz], pb[x, ry, rz], pc[x, ry, rz]
                slopes = (a2 - a0, b0 + b2 + 4.0 * b1, c0 + c2 + 4.0 * c1)
                a1, a2, b1, b2, c1, c2 = a0, a1, b0, b1, c0, c1
                pa[x + 2, ry, rz] = slopes[0]
                pb[x + 2, ry, rz] = slopes[1]
                pc[x + 2, ry, rz] = slopes[2]
                here = [here[c] - step[c] for c in range(3)]
                w = image[x + 1, ry, rz] + (here[0] * slopes[0] + here[1] * slopes[1] + here[2] * slopes[2])
                t = target[x, ry, rz]
                sw = sw + w
                sww = sww + w * w
                terms = [s * t for s in slopes] + list(slopes) + [s * w for s in slopes]
                if i > 0:
                    sums = [(s0 + f, s1 + (s0 + f)) for (s0, s1), f in zip(sums, terms)]
                else:
                    sums = [(s0 + f, s1) for (s0, s1), f in zip(sums, terms)]
            finish(e, 0, sums, ry, rz)
            return sw, sww

        return body

    sums = (zt, zt)
    for e in (1, 0):
        sums = lax.fori_loop(0, chunks, pass_one(e), sums)
    sum_w, sum_ww = sums

    lane = iota((1, 128), 1)

    def whole_sum(v):
        return jnp.sum(jnp.sum(v, axis=0, keepdims=True), axis=1, keepdims=True)

    def stat_copy(it, peer):
        g, d = place(peer)
        return (
            remote(stats.at[it, me], stats.at[it, me], sem_ss.at[it, peer], sem_sr.at[it, me], g, d),
            remote(stats.at[it, peer], stats.at[it, peer], sem_ss.at[it, peer], sem_sr.at[it, peer], g, d),
        )

    def send_stats(it, values):
        line = jnp.zeros((1, 128), F32)
        for r, v in enumerate(values):
            line = jnp.where(lane == r, whole_sum(v), line)
        stats[it, me] = line

        def go(k, carry):
            stat_copy(it, lax.rem(me + k, total))[0].start()
            return carry

        lax.fori_loop(1, total, go, 0)

    def take_stats(it, kinds):
        def go(k, carry):
            out, arrive = stat_copy(it, lax.rem(me + k, total))
            out.wait_send()
            arrive.wait_recv()
            return carry

        lax.fori_loop(1, total, go, 0)
        line = jnp.sum(stats[it], axis=0)
        return [jnp.sum(jnp.where(lane == r, line, 0.0), axis=1, keepdims=True) for r in range(kinds)]

    z_of_t = iota((depth, 128), 0) + gi * depth
    hat_down = hat(z_of_t - E * iota((depth, 128), 1)).astype(BF16)
    r_out, y_in = iota((32, rows), 0), iota((32, rows), 1)
    hat_rows = []
    for n in range(3):
        node = r_out - n * nodes_y
        inside = (node >= 0) & (node < nodes_y)
        hat_rows.append(jnp.where(inside, hat(y_in - E * node), 0.0).astype(BF16))

    def gather_nodes(f, carry):
        out = jnp.zeros((32, 128), F32)
        for n in range(3):
            along = split_dot_left(field[3 * f + n], hat_down)
            out = out + split_dot_right(hat_rows[n], along)
        packs[f] = out * (1.0 / 72.0)
        return carry

    send_stats(0, (sum_t, sum_tt, sum_w, sum_ww))
    lax.fori_loop(0, 9, gather_nodes, 0)
    st, stt, sw, sww = take_stats(0, 4)
    mean_ref = st / count
    var_ref = stt / count - mean_ref * mean_ref
    mean_1 = sw / count
    var_1 = sww / count - mean_1 * mean_1
    ratio_1 = jnp.sqrt((var_ref + EPS) / (var_1 + EPS))
    for c in range(3):
        slab[c] = packs[c] - mean_ref * packs[3 + c] - ratio_1 * (packs[6 + c] - mean_1 * packs[3 + c])

    near = [(dg, dd) for dg in (-1, 0, 1) for dd in (-1, 0, 1) if (dg, dd) != (0, 0)]
    moves = []
    for s, (dg, dd) in enumerate(near):
        slot = near.index((-dg, -dd))
        copy = remote(slab, nbuf.at[slot], sem_ns.at[slot], sem_nr.at[slot], gi + dg, di + dd)
        moves.append((dg, dd, slot, copy))

        @pl.when(exists(dg, dd))
        def _(copy=copy):
            copy.start()

        @pl.when(jnp.logical_not(exists(-dg, -dd)))
        def _(slot=slot):
            nbuf[slot] = jnp.zeros((3, 32, 128), F32)

    for dg, dd, slot, copy in moves:

        @pl.when(exists(dg, dd))
        def _(copy=copy):
            copy.wait_send()

        @pl.when(exists(-dg, -dd))
        def _(copy=copy):
            copy.wait_recv()

    def node_rows(block, n):
        return block[n * nodes_y : (n + 1) * nodes_y, 0:nodes_z]

    for c in range(3):
        same = slab[c]
        for dg in (-1, 1):
            same = same + nbuf[near.index((dg, 0)), c]
        left = jnp.zeros((32, 128), F32)
        right = jnp.zeros((32, 128), F32)
        for dg in (-1, 0, 1):
            left = left + nbuf[near.index((dg, -1)), c]
            right = right + nbuf[near.index((dg, 1)), c]
        for n in range(3):
            force = node_rows(same, n)
            if n == 0:
                force = force + node_rows(left, 2)
            if n == 2:
                force = force + node_rows(right, 0)
            m = 3 * c + n
            nodes[16 * m : 16 * m + nodes_y, 0:nodes_z] = init[c, 2 * di + n] + precond[c, 2 * di + n] * force
    expand()

    mean_1t, mean_rt, ratio_1t = (jnp.broadcast_to(v, tile) for v in (mean_1, mean_ref, ratio_1))

    def pass_two(e):
        def body(q, carry):
            sv, svv, see, sev = carry
            ry, rz = chunk_at(q)
            here = [fine[3 * c + e + 1, ry, rz] for c in range(3)]
            step = [(here[c] - fine[3 * c + e, ry, rz]) * (1.0 / E) for c in range(3)]
            sums = [(zt, zt)] * 3
            for i in range(E - 1, -1, -1):
                x = E * e + i
                slopes = (pa[x + 2, ry, rz], pb[x + 2, ry, rz], pc[x + 2, ry, rz])
                here = [here[c] - step[c] for c in range(3)]
                w = image[x + 1, ry, rz] + (here[0] * slopes[0] + here[1] * slopes[1] + here[2] * slopes[2])
                v = w - mean_1t
                image[x + 1, ry, rz] = v
                r = target[x, ry, rz] - mean_rt - ratio_1t * v
                sv = sv + v
                svv = svv + v * v
                see = see + r * r
                sev = sev + r * v
                terms = [s * v for s in slopes]
                if i > 0:
                    sums = [(s0 + f, s1 + (s0 + f)) for (s0, s1), f in zip(sums, terms)]
                else:
                    sums = [(s0 + f, s1) for (s0, s1), f in zip(sums, terms)]
            finish(e, 6, sums, ry, rz)
            return sv, svv, see, sev

        return body

    sums = (zt, zt, zt, zt)
    for e in (1, 0):
        sums = lax.fori_loop(0, chunks, pass_two(e), sums)
    send_stats(1, sums)
    lax.fori_loop(6, 9, gather_nodes, 0)
    sv, svv, see, sev = take_stats(1, 4)
    drift = sv / count
    var_2 = svv / count - drift * drift
    ratio_2 = jnp.sqrt((var_ref + EPS) / (var_2 + EPS))
    change = ratio_1 - ratio_2
    level = ratio_2 * drift
    squares = (
        see / count + change * change * (svv / count) + level * level
        + 2.0 * change * (sev / count) - 2.0 * level * ratio_1 * drift + 2.0 * change * level * drift
    )
    misfit[...] = jnp.sqrt(jnp.maximum(squares, 0.0))

    for c in range(3):
        second = packs[c] - mean_ref * packs[3 + c] - ratio_2 * (packs[6 + c] - drift * packs[3 + c])
        gbuf[gi, c] = slab[c] + second

    def over_grp(kk):
        peer = lax.rem(gi + kk, grps)
        return (
            remote(gbuf.at[gi], gbuf.at[gi], sem_gs.at[peer], sem_gr.at[gi], peer, di),
            remote(gbuf.at[peer], gbuf.at[peer], sem_gs.at[peer], sem_gr.at[peer], peer, di),
        )

    def over_dev(kk):
        peer = lax.rem(di + kk, devs)
        return (
            remote(dbuf.at[di], dbuf.at[di], sem_ds.at[peer], sem_dr.at[di], gi, peer),
            remote(dbuf.at[peer], dbuf.at[peer], sem_ds.at[peer], sem_dr.at[peer], gi, peer),
        )

    def start_all(make, size):
        def go(kk, carry):
            make(kk)[0].start()
            return carry

        lax.fori_loop(1, size, go, 0)

    def wait_all(make, size):
        def go(kk, carry):
            out, arrive = make(kk)
            out.wait_send()
            arrive.wait_recv()
            return carry

        lax.fori_loop(1, size, go, 0)

    start_all(over_grp, grps)

    offset = mean_ref - level

    def final(x, carry):
        target[x] = target[x] - offset - ratio_2 * image[x + 1]
        return carry

    half = width // 2
    outs = [
        pltpu.make_async_copy(target.at[pl.ds(h * half, half)], res_hbm.at[pl.ds(h * half, half)], sem_out.at[h])
        for h in range(2)
    ]
    lax.fori_loop(0, half, final, 0)
    outs[0].start()
    wait_all(over_grp, grps)
    dbuf[di] = jnp.sum(gbuf[...], axis=0)
    start_all(over_dev, devs)
    lax.fori_loop(half, width, final, 0)
    outs[1].start()
    wait_all(over_dev, devs)

    def place_pair(d, carry):
        for c in range(3):
            block = dbuf[d, c]
            before = dbuf[jnp.maximum(d - 1, 0), c]
            first = node_rows(block, 0) + jnp.where(d > 0, node_rows(before, 2), 0.0)
            disp[c, 2 * d] = init[c, 2 * d] + precond[c, 2 * d] * first
            disp[c, 2 * d + 1] = init[c, 2 * d + 1] + precond[c, 2 * d + 1] * node_rows(block, 1)
        return carry

    lax.fori_loop(0, devs, place_pair, 0)
    for c in range(3):
        last = node_rows(dbuf[devs - 1, c], 2)
        disp[c, 2 * devs] = init[c, 2 * devs] + precond[c, 2 * devs] * last
    outs[0].wait()
    outs[1].wait()


def local(ref_volume, def_volume, shifts, init_disp, precond):
    width, rows, depth = ref_volume.shape
    devs, grps = lax.axis_size("dev"), lax.axis_size("grp")
    total = grps * devs
    faces = jnp.stack([def_volume[:, :, 0], def_volume[:, :, depth - 1]])
    vmem = pl.BlockSpec(memory_space=pltpu.VMEM)
    hbm = pl.BlockSpec(memory_space=pl.ANY)
    dma = pltpu.SemaphoreType.DMA
    volume = pltpu.VMEM((width, rows, depth), F32)
    padded = pltpu.VMEM((width + 2, rows, depth), F32)
    disp, residual, misfit = pl.pallas_call(
        functools.partial(kernel, grps, devs),
        out_shape=(
            jax.ShapeDtypeStruct(init_disp.shape, F32),
            jax.ShapeDtypeStruct((width, rows, depth), F32),
            jax.ShapeDtypeStruct((1, 1), F32),
        ),
        in_specs=[hbm, hbm, vmem, pl.BlockSpec(memory_space=pltpu.SMEM), vmem, vmem],
        out_specs=(vmem, hbm, vmem),
        scratch_shapes=[
            pltpu.VMEM((width, rows, depth), BF16),
            pltpu.VMEM((width + 2 * MARGIN, rows, depth), BF16),
            pltpu.VMEM((2, 3, width, rows), BF16),
            pltpu.VMEM((2, 3 * width, rows), F32),
            pltpu.VMEM((rows, 128), BF16),
            volume,
            padded, padded, padded, padded,
            pltpu.VMEM((27, rows, depth), F32),
            pltpu.VMEM((9, rows, depth), F32),
            pltpu.VMEM((144, 128), F32),
            pltpu.VMEM((depth, 2 * depth), BF16),
            pltpu.VMEM((128, 2 * depth), jnp.int32),
            pltpu.VMEM((3, 32, 128), F32),
            pltpu.VMEM((9, 32, 128), F32),
            pltpu.VMEM((2, total, 1, 128), F32),
            pltpu.VMEM((8, 3, 32, 128), F32),
            pltpu.VMEM((grps, 3, 32, 128), F32),
            pltpu.VMEM((devs, 3, 32, 128), F32),
            dma((2,)), dma((2,)), dma((2,)), dma((2, 3)), dma((2, 3)),
            dma((2, total)), dma((2, total)), dma((8,)), dma((8,)),
            dma((grps,)), dma((grps,)), dma((devs,)), dma((devs,)), dma((2,)),
        ],
        compiler_params=pltpu.CompilerParams(
            collective_id=0, has_side_effects=True, vmem_limit_bytes=56 * 1024 * 1024
        ),
        cost_estimate=pl.CostEstimate(flops=10**9, bytes_accessed=10**7, transcendentals=0),
    )(ref_volume, def_volume, faces, shifts, init_disp, precond)
    return disp, residual, misfit[0, 0]


def solution(mesh):
    placed = (P("dev", None, "grp"), P("dev", None, "grp"), P("grp", "dev"), P(), P())
    return jax.shard_map(
        local,
        mesh=mesh,
        in_specs=placed,
        out_specs=(P(), P("dev", None, "grp"), P()),
        check_vma=False,
    )
```

```python
import functools

import jax
import jax.numpy as jnp
from jax import lax
from jax.experimental import pallas as pl
from jax.experimental.pallas import tpu as pltpu
from jax.sharding import PartitionSpec as P

E = 16
SMAX = 8
MARGIN = SMAX + 1
SPAN = 32
EPS = 1e-06
F32 = jnp.float32
BF16 = jnp.bfloat16
HIGHEST = lax.Precision.HIGHEST
MESH = pl.DeviceIdType.MESH


def iota(shape, dim):
    return lax.broadcasted_iota(jnp.int32, shape, dim)


def dot(a, b):
    return jnp.dot(a, b, preferred_element_type=F32)


def split_dot_left(a, b):
    high = a.astype(BF16)
    low = (a - high.astype(F32)).astype(BF16)
    return dot(high, b) + dot(low, b)


def split_dot_right(a, b):
    high = b.astype(BF16)
    low = (b - high.astype(F32)).astype(BF16)
    return dot(a, high) + dot(a, low)


def hat(distance):
    return jnp.maximum(1.0 - jnp.abs(distance).astype(F32) / E, 0.0)


def kernel(
    grps, devs, ref_hbm, def_hbm, shifts, init, precond,
    disp, centred_hbm, scalars,
    ref_v, wide, faces, face_n, face_b, face_f, turned, target, pa, pb, pc, image, field, fine, nodes, bands, offs,
    downs, slab, packs, stats, nbuf, gbuf, dbuf,
    sem_loc, sem_hs, sem_hr, sem_fs, sem_fr, sem_ss, sem_sr, sem_ns, sem_nr, sem_gs, sem_gr, sem_ds, sem_dr, sem_out,
):
    width, rows, depth = ref_v.shape
    nodes_y, nodes_z = init.shape[1], init.shape[3]
    total = grps * devs
    count = float(total * width * rows * depth)
    gi, di = lax.axis_index("grp"), lax.axis_index("dev")
    me = gi * devs + di

    def place(peer):
        return (peer // devs, lax.rem(peer, devs))

    def exists(dg, dd):
        g, d = gi + dg, di + dd
        return (g >= 0) & (g < grps) & (d >= 0) & (d < devs)

    def remote(src, dst, ss, rs, g, d):
        return pltpu.make_async_remote_copy(
            src_ref=src, dst_ref=dst, send_sem=ss, recv_sem=rs, device_id=(g, d), device_id_type=MESH
        )

    load_def = pltpu.make_async_copy(def_hbm, wide.at[pl.ds(MARGIN, width)], sem_loc.at[0])
    load_ref = pltpu.make_async_copy(ref_hbm, ref_v, sem_loc.at[1])
    load_def.start()
    load_ref.start()

    barrier = pltpu.get_barrier_semaphore()

    def greet(k, carry):
        pl.semaphore_signal(barrier, inc=1, device_id=place(lax.rem(me + k, total)), device_id_type=MESH)
        return carry

    lax.fori_loop(1, total, greet, 0)
    load_def.wait()
    ends, at = iota((16, depth), 0), iota((16, depth), 1)
    pick_ends = jnp.where(((ends == 0) & (at == 0)) | ((ends == 1) & (at == depth - 1)), 1.0, 0.0).astype(BF16)

    def cut(q, carry):
        for i in range(8):
            x = 8 * q + i
            both = lax.dot_general(
                pick_ends, wide[MARGIN + x], (((1,), (1,)), ((), ())), preferred_element_type=F32
            )
            face_n[x] = both[0:2]
        return carry

    lax.fori_loop(0, width // 8, cut, 0)
    for side in range(2):
        faces[side] = face_n[:, side].astype(BF16)
    pl.semaphore_wait(barrier, total - 1)

    to_right = remote(
        def_hbm.at[pl.ds(width - MARGIN, MARGIN)], wide.at[pl.ds(0, MARGIN)],
        sem_hs.at[0], sem_hr.at[0], gi, di + 1,
    )
    to_left = remote(
        def_hbm.at[pl.ds(0, MARGIN)], wide.at[pl.ds(MARGIN + width, MARGIN)],
        sem_hs.at[1], sem_hr.at[1], gi, di - 1,
    )
    has_left, has_right = di > 0, di < devs - 1

    @pl.when(has_right)
    def _():
        to_right.start()

    @pl.when(has_left)
    def _():
        to_left.start()

    face_moves = []
    for dg in (1, -1):
        for dd in (-1, 0, 1):
            side = 0 if dg == 1 else 1
            slot = 1 - dd
            copy = remote(
                faces.at[1 - side], face_b.at[side, slot],
                sem_fs.at[side, slot], sem_fr.at[side, slot], gi + dg, di + dd,
            )
            face_moves.append((dg, dd, copy))

            @pl.when(exists(dg, dd))
            def _(copy=copy):
                copy.start()

            @pl.when(jnp.logical_not(exists(-dg, -dd)))
            def _(side=side, slot=slot):
                face_b[side, slot] = jnp.zeros((width, rows), BF16)

    @pl.when(jnp.logical_not(has_left))
    def _():
        wide[pl.ds(0, MARGIN)] = jnp.zeros((MARGIN, rows, depth), BF16)

    @pl.when(jnp.logical_not(has_right))
    def _():
        wide[pl.ds(MARGIN + width, MARGIN)] = jnp.zeros((MARGIN, rows, depth), BF16)

    k, j = iota((depth, 2 * depth), 0), iota((depth, 2 * depth), 1)
    is_d = j >= depth
    gap = k - jnp.where(is_d, j - depth, j)
    smooth_w = jnp.where(gap == 0, 4.0, jnp.where(jnp.abs(gap) == 1, 1.0, 0.0))
    differ_w = jnp.where(jnp.abs(gap) == 1, gap, 0).astype(F32)
    bands[...] = jnp.where(is_d, differ_w, smooth_w).astype(BF16)
    k, j = iota((128, 2 * depth), 0), iota((128, 2 * depth), 1)
    low = (j == 0) | (j == depth)
    high = (j == depth - 1) | (j == 2 * depth - 1)
    offs[...] = jnp.where(low, k, jnp.where(high, k - 64, -1))

    nodes[...] = jnp.zeros_like(nodes)
    z_of = iota((128, depth), 1) + gi * depth
    hat_up = hat(z_of - E * iota((128, depth), 0))
    hat_y = hat(iota((rows, 16), 0) - E * iota((rows, 16), 1))

    def expand():
        along_z = jnp.dot(nodes[...], hat_up, preferred_element_type=F32, precision=HIGHEST) * (1.0 / 72.0)
        for m in range(9):
            fine[m] = jnp.dot(
                hat_y, along_z[16 * m : 16 * m + 16], preferred_element_type=F32, precision=HIGHEST
            )

    for c in range(3):
        for n in range(3):
            m = 3 * c + n
            nodes[16 * m : 16 * m + nodes_y, 0:nodes_z] = init[2 * di + n, :, c]
    expand()

    load_ref.wait()

    def convert(x, carry):
        s0, s1 = carry
        t = ref_v[x].astype(F32)
        target[x] = t
        t = t.reshape(rows // 8, 8, depth)
        return s0 + jnp.sum(t, axis=0), s1 + jnp.sum(t * t, axis=0)

    zero = jnp.zeros((8, depth), F32)
    sum_t, sum_tt = lax.fori_loop(0, width, convert, (zero, zero))


    @pl.when(has_right)
    def _():
        to_right.wait_send()
        to_left.wait_recv()

    @pl.when(has_left)
    def _():
        to_left.wait_send()
        to_right.wait_recv()

    for dg, dd, copy in face_moves:

        @pl.when(exists(dg, dd))
        def _(copy=copy):
            copy.wait_send()

        @pl.when(exists(-dg, -dd))
        def _(copy=copy):
            copy.wait_recv()

    shift = shifts[0, 0]
    for side in range(2):
        for slot in range(3):
            face_f[side, pl.ds(slot * width, width)] = face_b[side, slot].astype(F32)
    low_rows = face_f[0, pl.ds(width - 1 + shift, 40)]
    high_rows = face_f[1, pl.ds(width - 1 + shift, 40)]
    gap_rows = jnp.zeros((24, rows), F32)
    stacked = jnp.concatenate([low_rows, gap_rows, high_rows, gap_rows], axis=0)
    turned[...] = jnp.transpose(stacked).astype(BF16)

    row = iota((rows, depth), 0)
    column = iota((128, 2 * depth), 1)
    sign = jnp.where(column == depth, -1.0, 1.0)

    def gradient(x, carry):
        plane = wide[x + shift + SMAX]
        pick = jnp.where(offs[...] == x, sign, 0.0).astype(BF16)
        both = dot(plane, bands[...]) + dot(turned[...], pick)
        sz, dz = both[:, :depth], both[:, depth:]
        s_prev = jnp.where(row == 0, 0.0, pltpu.roll(sz, 1, 0))
        s_next = jnp.where(row == rows - 1, 0.0, pltpu.roll(sz, rows - 1, 0))
        d_prev = jnp.where(row == 0, 0.0, pltpu.roll(dz, 1, 0))
        d_next = jnp.where(row == rows - 1, 0.0, pltpu.roll(dz, rows - 1, 0))
        pa[x] = s_prev + s_next + 4.0 * sz
        pb[x] = s_next - s_prev
        pc[x] = d_prev + d_next + 4.0 * dz
        image[x] = plane.astype(F32)
        return carry

    lax.fori_loop(0, width + 2, gradient, 0)

    tile = (8, 128)
    lanes = depth // 128
    chunks = (rows // 8) * lanes

    def chunk_at(q):
        return pl.ds(pl.multiple_of((q // lanes) * 8, 8), 8), pl.ds(pl.multiple_of(lax.rem(q, lanes) * 128, 128), 128)

    def finish(e, base, sums, ry, rz):
        for m, (s0, s1) in enumerate(sums):
            s1 = s1 * (1.0 / E)
            f = base + m
            if e == 1:
                field[3 * f + 2, ry, rz] = s1
                field[3 * f + 1, ry, rz] = s0 - s1
            else:
                field[3 * f + 1, ry, rz] += s1
                field[3 * f, ry, rz] = s0 - s1

    zt = jnp.zeros(tile, F32)

    def pass_one(e):
        def body(q, carry):
            sw, sww = carry
            ry, rz = chunk_at(q)
            here = [fine[3 * c + e + 1, ry, rz] for c in range(3)]
            step = [(here[c] - fine[3 * c + e, ry, rz]) * (1.0 / E) for c in range(3)]
            sums = [(zt, zt)] * 9
            top = E * e + E + 1
            a1, a2 = pa[top - 1, ry, rz], pa[top, ry, rz]
            b1, b2 = pb[top - 1, ry, rz], pb[top, ry, rz]
            c1, c2 = pc[top - 1, ry, rz], pc[top, ry, rz]
            for i in range(E - 1, -1, -1):
                x = E * e + i
                a0, b0, c0 = pa[x, ry, rz], pb[x, ry, rz], pc[x, ry, rz]
                slopes = (a2 - a0, b0 + b2 + 4.0 * b1, c0 + c2 + 4.0 * c1)
                a1, a2, b1, b2, c1, c2 = a0, a1, b0, b1, c0, c1
                pa[x + 2, ry, rz] = slopes[0]
                pb[x + 2, ry, rz] = slopes[1]
                pc[x + 2, ry, rz] = slopes[2]
                here = [here[c] - step[c] for c in range(3)]
                w = image[x + 1, ry, rz] + (here[0] * slopes[0] + here[1] * slopes[1] + here[2] * slopes[2])
                t = target[x, ry, rz]
                sw = sw + w
                sww = sww + w * w
                terms = [s * t for s in slopes] + list(slopes) + [s * w for s in slopes]
                if i > 0:
                    sums = [(s0 + f, s1 + (s0 + f)) for (s0, s1), f in zip(sums, terms)]
                else:
                    sums = [(s0 + f, s1) for (s0, s1), f in zip(sums, terms)]
            finish(e, 0, sums, ry, rz)
            return sw, sww

        return body

    sums = (zt, zt)
    for e in (1, 0):
        sums = lax.fori_loop(0, chunks, pass_one(e), sums)
    sum_w, sum_ww = sums

    lane = iota((1, 128), 1)

    def whole_sum(v):
        return jnp.sum(jnp.sum(v, axis=0, keepdims=True), axis=1, keepdims=True)

    def stat_copy(it, peer):
        g, d = place(peer)
        return (
            remote(stats.at[it, me], stats.at[it, me], sem_ss.at[it, peer], sem_sr.at[it, me], g, d),
            remote(stats.at[it, peer], stats.at[it, peer], sem_ss.at[it, peer], sem_sr.at[it, peer], g, d),
        )

    def send_stats(it, values):
        line = jnp.zeros((1, 128), F32)
        for r, v in enumerate(values):
            line = jnp.where(lane == r, whole_sum(v), line)
        stats[it, me] = line

        def go(k, carry):
            stat_copy(it, lax.rem(me + k, total))[0].start()
            return carry

        lax.fori_loop(1, total, go, 0)

    def take_stats(it, kinds):
        def go(k, carry):
            out, arrive = stat_copy(it, lax.rem(me + k, total))
            out.wait_send()
            arrive.wait_recv()
            return carry

        lax.fori_loop(1, total, go, 0)
        line = jnp.sum(stats[it], axis=0)
        return [jnp.sum(jnp.where(lane == r, line, 0.0), axis=1, keepdims=True) for r in range(kinds)]

    lane_t = iota((depth, 128), 1)
    local_node = lane_t % SPAN
    hat_down = jnp.where(local_node <= depth // E, hat(iota((depth, 128), 0) - E * local_node), 0.0)
    for c in range(3):
        downs[c] = jnp.where(lane_t // SPAN == c, hat_down, 0.0).astype(BF16)
    r_out, y_in = iota((32, rows), 0), iota((32, rows), 1)
    hat_rows = []
    for n in range(3):
        node = r_out - n * nodes_y
        inside = (node >= 0) & (node < nodes_y)
        hat_rows.append(jnp.where(inside, hat(y_in - E * node), 0.0).astype(BF16))

    def gather_nodes(kind, carry):
        out = jnp.zeros((32, 128), F32)
        for n in range(3):
            along = jnp.zeros((rows, 128), F32)
            for c in range(3):
                along = along + split_dot_left(field[9 * kind + 3 * c + n], downs[c])
            out = out + split_dot_right(hat_rows[n], along)
        packs[kind] = out * (1.0 / 72.0)
        return carry

    send_stats(0, (sum_t, sum_tt, sum_w, sum_ww))
    lax.fori_loop(0, 3, gather_nodes, 0)
    st, stt, sw, sww = take_stats(0, 4)
    mean_ref = st / count
    var_ref = stt / count - mean_ref * mean_ref
    mean_1 = sw / count
    var_1 = sww / count - mean_1 * mean_1
    ratio_1 = jnp.sqrt((var_ref + EPS) / (var_1 + EPS))
    slab[...] = packs[0] - mean_ref * packs[1] - ratio_1 * (packs[2] - mean_1 * packs[1])

    near = [(dg, dd) for dg in (-1, 0, 1) for dd in (-1, 0, 1) if (dg, dd) != (0, 0)]
    moves = []
    for s, (dg, dd) in enumerate(near):
        slot = near.index((-dg, -dd))
        copy = remote(slab, nbuf.at[slot], sem_ns.at[slot], sem_nr.at[slot], gi + dg, di + dd)
        moves.append((dg, dd, slot, copy))

        @pl.when(exists(dg, dd))
        def _(copy=copy):
            copy.start()

        @pl.when(jnp.logical_not(exists(-dg, -dd)))
        def _(slot=slot):
            nbuf[slot] = jnp.zeros((32, 128), F32)

    for dg, dd, slot, copy in moves:

        @pl.when(exists(dg, dd))
        def _(copy=copy):
            copy.wait_send()

        @pl.when(exists(-dg, -dd))
        def _(copy=copy):
            copy.wait_recv()

    def node_rows(block, n):
        return block[n * nodes_y : (n + 1) * nodes_y, 0:nodes_z]

    lane_b = iota((32, 128), 1) % SPAN
    last = depth // E

    def joined(middle, dd):
        below = pltpu.roll(nbuf[near.index((-1, dd))], 128 - last, 1)
        above = pltpu.roll(nbuf[near.index((1, dd))], last, 1)
        return middle + jnp.where(lane_b == 0, below, jnp.where(lane_b == last, above, 0.0))

    from_k, to_k = iota((128, 128), 0), iota((128, 128), 1) - gi * last
    for c in range(3):
        fits = (to_k >= 0) & (to_k <= last) & (from_k == to_k + SPAN * c)
        spread = jnp.where(fits, 1.0, 0.0)
        same, left, right = (
            jnp.dot(block, spread, preferred_element_type=F32, precision=HIGHEST)
            for block in (
                joined(slab[...], 0),
                joined(nbuf[near.index((0, -1))], -1),
                joined(nbuf[near.index((0, 1))], 1),
            )
        )
        for n in range(3):
            force = node_rows(same, n)
            if n == 0:
                force = force + node_rows(left, 2)
            if n == 2:
                force = force + node_rows(right, 0)
            m = 3 * c + n
            nodes[16 * m : 16 * m + nodes_y, 0:nodes_z] = init[2 * di + n, :, c] + precond[2 * di + n, :, c] * force
    expand()

    mean_1t, mean_rt, ratio_1t = (jnp.broadcast_to(v, tile) for v in (mean_1, mean_ref, ratio_1))

    def pass_two(e):
        def body(q, carry):
            sv, svv, see, sev = carry
            ry, rz = chunk_at(q)
            here = [fine[3 * c + e + 1, ry, rz] for c in range(3)]
            step = [(here[c] - fine[3 * c + e, ry, rz]) * (1.0 / E) for c in range(3)]
            sums = [(zt, zt)] * 3
            for i in range(E - 1, -1, -1):
                x = E * e + i
                slopes = (pa[x + 2, ry, rz], pb[x + 2, ry, rz], pc[x + 2, ry, rz])
                here = [here[c] - step[c] for c in range(3)]
                w = image[x + 1, ry, rz] + (here[0] * slopes[0] + here[1] * slopes[1] + here[2] * slopes[2])
                v = w - mean_1t
                image[x + 1, ry, rz] = v
                r = target[x, ry, rz] - mean_rt - ratio_1t * v
                sv = sv + v
                svv = svv + v * v
                see = see + r * r
                sev = sev + r * v
                terms = [s * v for s in slopes]
                if i > 0:
                    sums = [(s0 + f, s1 + (s0 + f)) for (s0, s1), f in zip(sums, terms)]
                else:
                    sums = [(s0 + f, s1) for (s0, s1), f in zip(sums, terms)]
            finish(e, 6, sums, ry, rz)
            return sv, svv, see, sev

        return body

    sums = (zt, zt, zt, zt)
    half = width // 2
    outs = [
        pltpu.make_async_copy(image.at[pl.ds(h * half + 1, half)], centred_hbm.at[pl.ds(h * half, half)], sem_out.at[h])
        for h in range(2)
    ]
    for e in (1, 0):
        sums = lax.fori_loop(0, chunks, pass_two(e), sums)
        outs[e].start()
    send_stats(1, sums)
    gather_nodes(2, 0)
    sv, svv, see, sev = take_stats(1, 4)
    drift = sv / count
    var_2 = svv / count - drift * drift
    ratio_2 = jnp.sqrt((var_ref + EPS) / (var_2 + EPS))
    change = ratio_1 - ratio_2
    level = ratio_2 * drift
    squares = (
        see / count + change * change * (svv / count) + level * level
        + 2.0 * change * (sev / count) - 2.0 * level * ratio_1 * drift + 2.0 * change * level * drift
    )
    line = jnp.where(lane == 0, mean_ref - level, jnp.where(lane == 1, ratio_2, jnp.sqrt(jnp.maximum(squares, 0.0))))
    scalars[...] = line

    second = packs[0] - mean_ref * packs[1] - ratio_2 * (packs[2] - drift * packs[1])
    dbuf[di] = slab[...] + second

    def over_grp(kk):
        peer = lax.rem(gi + kk, grps)
        return (
            remote(gbuf.at[gi], gbuf.at[gi], sem_gs.at[peer], sem_gr.at[gi], peer, di),
            remote(gbuf.at[peer], gbuf.at[peer], sem_gs.at[peer], sem_gr.at[peer], peer, di),
        )

    def over_dev(kk):
        peer = lax.rem(di + kk, devs)
        return (
            remote(dbuf.at[di], dbuf.at[di], sem_ds.at[peer], sem_dr.at[di], gi, peer),
            remote(dbuf.at[peer], dbuf.at[peer], sem_ds.at[peer], sem_dr.at[peer], gi, peer),
        )

    def start_all(make, size):
        def go(kk, carry):
            make(kk)[0].start()
            return carry

        lax.fori_loop(1, size, go, 0)

    def wait_all(make, size):
        def go(kk, carry):
            out, arrive = make(kk)
            out.wait_send()
            arrive.wait_recv()
            return carry

        lax.fori_loop(1, size, go, 0)

    start_all(over_dev, devs)
    wait_all(over_dev, devs)
    for d in range(devs):
        block = dbuf[d]
        first = block[0:nodes_y]
        if d > 0:
            first = first + dbuf[d - 1][2 * nodes_y : 3 * nodes_y]
        gbuf[gi, 2 * d * nodes_y : (2 * d + 1) * nodes_y] = first
        gbuf[gi, (2 * d + 1) * nodes_y : (2 * d + 2) * nodes_y] = block[nodes_y : 2 * nodes_y]
    gbuf[gi, 2 * devs * nodes_y : (2 * devs + 1) * nodes_y] = dbuf[devs - 1][2 * nodes_y : 3 * nodes_y]
    gbuf[gi, (2 * devs + 1) * nodes_y :] = jnp.zeros((gbuf.shape[1] - (2 * devs + 1) * nodes_y, 128), F32)
    start_all(over_grp, grps)
    wait_all(over_grp, grps)
    spot = iota((gbuf.shape[1], 128), 1)
    for c in range(3):
        force = jnp.zeros((gbuf.shape[1], 128), F32)
        for g in range(grps):
            moved = pltpu.roll(gbuf[g], (g * last - SPAN * c) % 128, 1)
            force = force + jnp.where((spot >= g * last) & (spot <= (g + 1) * last), moved, 0.0)
        for n in range(2 * devs + 1):
            disp[n, :, c] = init[n, :, c] + precond[n, :, c] * force[n * nodes_y : (n + 1) * nodes_y, 0:nodes_z]
    outs[0].wait()
    outs[1].wait()


def local(ref_volume, def_volume, shifts, init_disp, precond):
    width, rows, depth = ref_volume.shape
    devs, grps = lax.axis_size("dev"), lax.axis_size("grp")
    total = grps * devs
    gather_rows = -(-init_disp.shape[1] * init_disp.shape[2] // 8) * 8
    init_t, precond_t = (jnp.transpose(a, (1, 2, 0, 3)) for a in (init_disp, precond))
    vmem = pl.BlockSpec(memory_space=pltpu.VMEM)
    hbm = pl.BlockSpec(memory_space=pl.ANY)
    dma = pltpu.SemaphoreType.DMA
    volume = pltpu.VMEM((width, rows, depth), F32)
    padded = pltpu.VMEM((width + 2, rows, depth), F32)
    disp, centred, scalars = pl.pallas_call(
        functools.partial(kernel, grps, devs),
        out_shape=(
            jax.ShapeDtypeStruct(init_t.shape, F32),
            jax.ShapeDtypeStruct((width, rows, depth), F32),
            jax.ShapeDtypeStruct((1, 128), F32),
        ),
        in_specs=[hbm, hbm, pl.BlockSpec(memory_space=pltpu.SMEM), vmem, vmem],
        out_specs=(vmem, hbm, vmem),
        scratch_shapes=[
            pltpu.VMEM((width, rows, depth), BF16),
            pltpu.VMEM((width + 2 * MARGIN, rows, depth), BF16),
            pltpu.VMEM((2, width, rows), BF16),
            pltpu.VMEM((width, 2, rows), F32),
            pltpu.VMEM((2, 3, width, rows), BF16),
            pltpu.VMEM((2, 3 * width, rows), F32),
            pltpu.VMEM((rows, 128), BF16),
            volume,
            padded, padded, padded, padded,
            pltpu.VMEM((27, rows, depth), F32),
            pltpu.VMEM((9, rows, depth), F32),
            pltpu.VMEM((144, 128), F32),
            pltpu.VMEM((depth, 2 * depth), BF16),
            pltpu.VMEM((128, 2 * depth), jnp.int32),
            pltpu.VMEM((3, depth, 128), BF16),
            pltpu.VMEM((32, 128), F32),
            pltpu.VMEM((3, 32, 128), F32),
            pltpu.VMEM((2, total, 1, 128), F32),
            pltpu.VMEM((8, 32, 128), F32),
            pltpu.VMEM((grps, gather_rows, 128), F32),
            pltpu.VMEM((devs, 32, 128), F32),
            dma((2,)), dma((2,)), dma((2,)), dma((2, 3)), dma((2, 3)),
            dma((2, total)), dma((2, total)), dma((8,)), dma((8,)),
            dma((grps,)), dma((grps,)), dma((devs,)), dma((devs,)), dma((2,)),
        ],
        compiler_params=pltpu.CompilerParams(
            collective_id=0, has_side_effects=True, vmem_limit_bytes=56 * 1024 * 1024
        ),
        cost_estimate=pl.CostEstimate(flops=10**9, bytes_accessed=10**7, transcendentals=0),
    )(ref_volume, def_volume, shifts, init_t, precond_t)
    offset, ratio, misfit = scalars[0, 0], scalars[0, 1], scalars[0, 2]
    residual = ref_volume.astype(F32) - offset - ratio * centred
    return jnp.transpose(disp, (2, 0, 1, 3)), residual, misfit


def solution(mesh):
    placed = (P("dev", None, "grp"), P("dev", None, "grp"), P("grp", "dev"), P(), P())
    return jax.shard_map(
        local,
        mesh=mesh,
        in_specs=placed,
        out_specs=(P(), P("dev", None, "grp"), P()),
        check_vma=False,
    )
```
